256 devices in a mesh: node: 8 (over z_hi, core), group: 32 (over x, y, z_lo).
Axes of the slice: x: 4, y: 4, z: 8 (z_hi: 4, z_lo: 2; z = z_hi * 2 + z_lo), core: 2. Of those that a mesh axis runs over, the one named last changes fastest.
Arguments:
- grads: float32 [256, 3145728], P(('node', 'group')), may hold values from -1.5 to 1.5
Outputs:
- reduced: float32 [3145728], P(('node', 'group'))
The draws below stay inside these ranges and needn't reach their ends.
All inputs are finite; a program needn't handle non-finite values. Where the reference program divides by a largest or mean magnitude, that divisor is 1e-20 or more.
Results may differ from the reference program's by a relative error of at most 0.0041.
Values may be sent and summed in bfloat16 or wider, within the bound.
No kernel may reach another device: no remote copies, remote signals or barrier semaphores. Data moves between devices by JAX's collectives and lax.ppermute only.
A program may use at most 128 MiB of HBM per device.

```python
import jax
import jax.numpy as jnp
from jax import lax

NB = 96
QB = 128
L = 3145728
N_NODE = 8
N_GROUP = 32
DEVICES = 256


def strengthened(entries, rng, source, target, shards_of, factor):
    owner, partner = [(jnp.arange(entries.shape[position]) // (entries.shape[position] // shards_of)).reshape([-1 if axis == position else 1 for axis in range(entries.ndim)]) for position in (source, target)]
    chosen = jax.random.permutation(rng, shards_of)[partner]
    strong = (owner == chosen) | (owner == (partner + shards_of // 2) % shards_of)
    return jnp.where(strong, factor * entries, entries)


def level_of(rng, shape, pieces, smallest, high):
    def one(axis_at, shards_of):
        heights = jax.random.uniform(jax.random.fold_in(jax.random.fold_in(rng, 6), axis_at), (shards_of,), jnp.float32, smallest / len(pieces), high / len(pieces))
        return jnp.repeat(jnp.exp(heights), shape[axis_at] // shards_of).reshape((-1,) + (1,) * (len(shape) - axis_at - 1))

    gain = one(*pieces[0])
    for cut in pieces[1:]:
        gain = gain * one(*cut)
    return gain


def gaussian_with(key, extent, scale, bound, pieces, heavy, held_as=jnp.bfloat16):
    array = scale * jax.random.normal(key, extent, jnp.float32)
    if pieces:
        array = array * level_of(key, extent, pieces, -0.22, 0.18)
    return jnp.clip(strengthened(array, jax.random.fold_in(key, 3), *heavy), -bound, bound).astype(held_as)


def setup_inputs(seed: int = 0) -> dict:
    seeds = jax.random.split(jax.random.key(seed), 2)
    grads = gaussian_with(seeds[0], (DEVICES, L), 0.0625, 1.5, ((0, 256),), (0, 1, 256, 6.0), jnp.float32)
    return dict(grads=grads)


EPS = 1e-6


def quantize(values):
    scales = (jnp.max(jnp.abs(values), axis=-1) + EPS).astype(jnp.bfloat16)
    scales = lax.optimization_barrier(scales)
    quant = (values / scales.astype(jnp.float32)[..., None]).astype(jnp.bfloat16)
    return lax.optimization_barrier((quant, scales))


def expand(quant, scales):
    return quant.astype(jnp.float32) * scales.astype(jnp.float32)[..., None]


def reference(grads):
    shaped = grads.reshape(N_NODE, N_GROUP, N_NODE, N_GROUP, NB, QB)

    def per_group(total, member):
        slab = lax.dynamic_index_in_dim(shaped, member, 1, keepdims=False)
        quant, scales = quantize(slab)
        partial_value = jnp.sum(expand(quant, scales), axis=0)
        quant_two, scales_two = quantize(partial_value)
        return total + expand(quant_two, scales_two), None

    start = jnp.zeros((N_NODE, N_GROUP, NB, QB), jnp.float32)
    total, unused = lax.scan(per_group, start, jnp.arange(N_GROUP, dtype=jnp.int32))
    return total.reshape(-1)
```

```python
import functools

import jax
import jax.numpy as jnp
from jax import lax
from jax.experimental import pallas as pl
from jax.experimental.pallas import tpu as pltpu
from jax.sharding import PartitionSpec as P

QB = 128
ZH, CORE, X, Y, ZL = 4, 2, 4, 4, 2
RING = 4
BF16, F32 = jnp.bfloat16, jnp.float32


def flat(zh, c, x, y, zl):
    return (((zh * CORE + c) * X + x) * Y + y) * ZL + zl


def permutation(move):
    pairs = []
    for zh in range(ZH):
        for c in range(CORE):
            for x in range(X):
                for y in range(Y):
                    for zl in range(ZL):
                        pairs.append((flat(zh, c, x, y, zl), flat(*move(zh, c, x, y, zl))))
    return pairs


def to_other_core(values):
    return lax.ppermute(values, ("node", "group"), permutation(lambda zh, c, x, y, zl: (zh, 1 - c, x, y, zl)))


def along(values, shift, first):
    def move(zh, c, x, y, zl):
        if (c == 0) == first:
            return zh, c, (x + shift) % X, y, zl
        return zh, c, x, (y + shift) % Y, zl

    return lax.ppermute(values, ("node", "group"), permutation(move))


def z_groups():
    groups = []
    for c in range(CORE):
        for x in range(X):
            for y in range(Y):
                groups.append([flat(zh, c, x, y, zl) for zh in range(ZH) for zl in range(ZL)])
    return groups


def fetch(place, grads, held, sems):
    core, first = place[0], place[1]
    copies = []
    for zh in range(ZH):
        for other in range(RING):
            x = jnp.where(core == 0, first, other)
            y = jnp.where(core == 0, other, first)
            copy = pltpu.make_async_copy(grads.at[zh, core, x, y], held.at[zh, other], sems.at[zh, other])
            copy.start()
            copies.append((zh, other, copy))
    return copies


def cast_kernel(place, grads, out, held, sems):
    for zh, other, copy in fetch(place, grads, held, sems):
        copy.wait()
        out[zh, other] = held[zh, other].astype(BF16)


def add_kernel(place, grads, received, out, held, sems):
    for zh, other, copy in fetch(place, grads, held, sems):
        copy.wait()
        out[zh, other] = (held[zh, other] + received[zh, other].astype(F32)).astype(BF16)


def first_sum_kernel(place, grads, r0, p1, p2, p3, own, o1, o2, o3, held, sems):
    for zh, other, copy in fetch(place, grads, held, sems):
        copy.wait()
        total = held[zh, other] + r0[zh, other].astype(F32)
        total += p1[zh, other].astype(F32) + p2[zh, other].astype(F32) + p3[zh, other].astype(F32)
        held[zh, other] = total
    second = place[2]
    own[...] = held[:, second]
    for t, out in ((1, o1), (2, o2), (3, o3)):
        out[...] = held[:, lax.rem(second + t, RING)].astype(BF16)


def second_sum_kernel(own, u1, u2, u3, out):
    out[...] = (own[...] + u1[...].astype(F32) + u2[...].astype(F32) + u3[...].astype(F32)).astype(BF16)


def last_sum_kernel(pieces, out):
    out[...] = jnp.sum(pieces[...].astype(F32), axis=0)


VMEM = pl.BlockSpec(memory_space=pltpu.VMEM)


def call(kernel, out_shape, place, grads, *others):
    rows, lanes = grads.shape[-2:]
    return pl.pallas_call(
        kernel,
        out_shape=out_shape,
        in_specs=[pl.BlockSpec(memory_space=pltpu.SMEM), pl.BlockSpec(memory_space=pltpu.HBM)] + [VMEM] * len(others),
        out_specs=jax.tree.map(lambda _: VMEM, out_shape),
        scratch_shapes=[pltpu.VMEM((ZH, RING, rows, lanes), F32), pltpu.SemaphoreType.DMA((ZH, RING))],
        compiler_params=pltpu.CompilerParams(vmem_limit_bytes=32 * 1024 * 1024),
        cost_estimate=pl.CostEstimate(flops=ZH * RING * rows * lanes, bytes_accessed=ZH * RING * rows * lanes * 6, transcendentals=0),
    )(place, pltpu.with_memory_space_constraint(grads, pltpu.HBM), *others)


def on_device(grads):
    blocks = grads.shape[1] // (ZH * CORE * X * Y * ZL * QB)
    rows = ZL * blocks
    grads = grads.reshape(ZH, CORE, X, Y, rows, QB)
    node, group = lax.axis_index("node"), lax.axis_index("group")
    core = node % CORE
    x, y = group // (Y * ZL), (group // ZL) % Y
    first, second = jnp.where(core == 0, x, y), jnp.where(core == 0, y, x)

    def place_of(core, first, second):
        return jnp.stack([core, first, second]).astype(jnp.int32)

    quarter = jax.ShapeDtypeStruct((ZH, RING, rows, QB), BF16)
    crossed = {}
    for shift in (2, 1, 3, 0):
        mine = call(cast_kernel, quarter, place_of(1 - core, (second + shift) % RING, first), grads)
        crossed[shift] = to_other_core(mine)
    arrived = []
    for shift in (2, 1, 3):
        summed = call(add_kernel, quarter, place_of(core, (first + shift) % RING, second), grads, crossed[shift])
        arrived.append(along(summed, shift, True))
    piece = (ZH, rows, QB)
    own, *outs = call(
        first_sum_kernel,
        [jax.ShapeDtypeStruct(piece, F32)] + [jax.ShapeDtypeStruct(piece, BF16)] * 3,
        place_of(core, first, second),
        grads,
        crossed[0],
        *arrived,
    )
    got = {}
    for shift in (2, 1, 3):
        got[shift] = along(outs[shift - 1], shift, False)
    total = pl.pallas_call(second_sum_kernel, out_shape=jax.ShapeDtypeStruct(piece, BF16))(own, got[1], got[2], got[3])
    pieces = lax.all_to_all(
        total.reshape(ZH * ZL, blocks, QB), ("node", "group"), 0, 0, axis_index_groups=z_groups(), tiled=True
    )
    out = pl.pallas_call(last_sum_kernel, out_shape=jax.ShapeDtypeStruct((blocks, QB), F32))(pieces)
    return out.reshape(blocks * QB)


def solution(mesh):
    placed = (P(("node", "group"), None),)
    return jax.shard_map(
        on_device, mesh=mesh, in_specs=placed, out_specs=P(("node", "group")), check_vma=False
    )
```

```python
import functools

import jax
import jax.numpy as jnp
from jax import lax
from jax.experimental import pallas as pl
from jax.experimental.pallas import tpu as pltpu
from jax.sharding import PartitionSpec as P

QB = 128
ZH, CORE, X, Y, ZL = 4, 2, 4, 4, 2
RING = 4
COST = 0
AXES = ("node", "group")
BF16, F32 = jnp.bfloat16, jnp.float32


def flat(zh, c, x, y, zl):
    return (((zh * CORE + c) * X + x) * Y + y) * ZL + zl


def permuted(values, move):
    pairs = []
    for zh in range(ZH):
        for c in range(CORE):
            for x in range(X):
                for y in range(Y):
                    for zl in range(ZL):
                        pairs.append((flat(zh, c, x, y, zl), flat(*move(zh, c, x, y, zl))))
    return lax.ppermute(values, AXES, pairs)


def to_other_core(values):
    return permuted(values, lambda zh, c, x, y, zl: (zh, 1 - c, x, y, zl))


def along(values, shift, first):
    def move(zh, c, x, y, zl):
        if (c == 0) == first:
            return zh, c, (x + shift) % X, y, zl
        return zh, c, x, (y + shift) % Y, zl

    return permuted(values, move)


def z_groups():
    groups = []
    for c in range(CORE):
        for x in range(X):
            for y in range(Y):
                groups.append([flat(zh, c, x, y, zl) for zh in range(ZH) for zl in range(ZL)])
    return groups


def place():
    node, group = lax.axis_index("node"), lax.axis_index("group")
    core = lax.rem(node, CORE)
    x, y = lax.div(group, Y * ZL), lax.rem(lax.div(group, ZL), Y)
    return core, jnp.where(core == 0, x, y), jnp.where(core == 0, y, x)


def steps_kernel(steps, grads, *refs):
    n_received = sum(added for _, added in steps)
    received, outs = list(refs[:n_received]), refs[n_received : n_received + len(steps)]
    held, sems = refs[n_received + len(steps) :]
    core, first, second = place()
    copies = []
    for k, (shift, added) in enumerate(steps):
        half = core if added else 1 - core
        at = lax.rem((first if added else second) + shift, RING)
        for zh in range(ZH):
            for other in range(RING):
                x, y = jnp.where(half == 0, at, other), jnp.where(half == 0, other, at)
                copy = pltpu.make_async_copy(grads.at[zh, half, x, y], held.at[k, zh, other], sems.at[k, zh, other])
                copy.start()
                copies.append(copy)
    copies = iter(copies)
    for k, (_, added) in enumerate(steps):
        source = received.pop(0) if added else None
        for zh in range(ZH):
            for other in range(RING):
                next(copies).wait()
                value = held[k, zh, other]
                if added:
                    value += source[zh, other].astype(F32)
                outs[k][zh, other] = value.astype(outs[k].dtype)


VMEM = pl.BlockSpec(memory_space=pltpu.VMEM)


def run_steps(grads, steps, received=(), dtype=BF16):
    rows, lanes = grads.shape[-2:]
    size = len(steps) * ZH * RING * rows * lanes
    return pl.pallas_call(
        functools.partial(steps_kernel, steps),
        out_shape=[pltpu.VMEM((ZH, RING, rows, lanes), dtype)] * len(steps),
        in_specs=[pl.BlockSpec(memory_space=pltpu.HBM)] + [VMEM] * len(received),
        out_specs=[VMEM] * len(steps),
        scratch_shapes=[
            pltpu.VMEM((len(steps), ZH, RING, rows, lanes), F32),
            pltpu.SemaphoreType.DMA((len(steps), ZH, RING)),
        ],
        compiler_params=pltpu.CompilerParams(vmem_limit_bytes=10 * 1024 * 1024),
        cost_estimate=pl.CostEstimate(flops=COST, bytes_accessed=COST, transcendentals=0),
    )(pltpu.with_memory_space_constraint(grads, pltpu.HBM), *received)


def on_device(grads):
    blocks = grads.shape[1] // (ZH * CORE * X * Y * ZL * QB)
    grads = grads.reshape(ZH, CORE, X, Y, ZL * blocks, QB)
    second = place()[2]

    (c2,) = run_steps(grads, ((2, False),))
    later = lax.optimization_barrier((grads, c2))[0]
    c1, c3, c0 = run_steps(later, ((1, False), (3, False), (0, False)))
    c2, c1, c3, c0 = [to_other_core(c) for c in (c2, c1, c3, c0)]
    (s2,) = run_steps(grads, ((2, True),), (c2,))
    p2 = along(s2, 2, True)
    grads = lax.optimization_barrier((grads, s2))[0]
    (s1,) = run_steps(grads, ((1, True),), (c1,))
    p1 = along(s1, 1, True)
    grads = lax.optimization_barrier((grads, s1))[0]
    (s3,) = run_steps(grads, ((3, True),), (c3,))
    p3 = along(s3, 3, True)
    grads = lax.optimization_barrier((grads, s3))[0]
    (s0,) = run_steps(grads, ((0, True),), (c0,), F32)

    total = s0 + p1.astype(F32) + p2.astype(F32) + p3.astype(F32)

    def piece(shift):
        return lax.dynamic_index_in_dim(total, lax.rem(second + shift, RING), 1, keepdims=False)

    summed = piece(0)
    for shift in (2, 1, 3):
        summed += along(piece(shift).astype(BF16), shift, False).astype(F32)
    pieces = summed.astype(BF16).reshape(ZH * ZL, blocks, QB)
    pieces = lax.all_to_all(pieces, AXES, 0, 0, axis_index_groups=z_groups(), tiled=True)
    return jnp.sum(pieces.astype(F32), axis=0).reshape(blocks * QB)


def solution(mesh):
    placed = (P(("node", "group"), None),)
    return jax.shard_map(
        on_device, mesh=mesh, in_specs=placed, out_specs=P(("node", "group")), check_vma=False
    )
```

```python
import functools

import jax
import jax.numpy as jnp
from jax import lax
from jax.experimental import pallas as pl
from jax.experimental.pallas import tpu as pltpu
from jax.sharding import PartitionSpec as P

QB = 128
ZH, CORE, X, Y, ZL = 4, 2, 4, 4, 2
RING = 4
AXES = ("node", "group")
BF16, F32 = jnp.bfloat16, jnp.float32


def flat(zh, c, x, y, zl):
    return (((zh * CORE + c) * X + x) * Y + y) * ZL + zl


def permuted(values, move):
    pairs = []
    for zh in range(ZH):
        for c in range(CORE):
            for x in range(X):
                for y in range(Y):
                    for zl in range(ZL):
                        pairs.append((flat(zh, c, x, y, zl), flat(*move(zh, c, x, y, zl))))
    return lax.ppermute(values, AXES, pairs)


def to_other_core(values):
    return permuted(values, lambda zh, c, x, y, zl: (zh, 1 - c, x, y, zl))


def along(values, shift, first):
    def move(zh, c, x, y, zl):
        if (c == 0) == first:
            return zh, c, (x + shift) % X, y, zl
        return zh, c, x, (y + shift) % Y, zl

    return permuted(values, move)


def z_groups():
    groups = []
    for c in range(CORE):
        for x in range(X):
            for y in range(Y):
                groups.append([flat(zh, c, x, y, zl) for zh in range(ZH) for zl in range(ZL)])
    return groups


def place():
    node, group = lax.axis_index("node"), lax.axis_index("group")
    core = lax.rem(node, CORE)
    x, y = lax.div(group, Y * ZL), lax.rem(lax.div(group, ZL), Y)
    return core, jnp.where(core == 0, x, y), jnp.where(core == 0, y, x)


def steps_kernel(steps, grads, *refs):
    n_received = sum(added for _, _, added in steps)
    received, outs = list(refs[:n_received]), refs[n_received : n_received + len(steps)]
    held, sems = refs[n_received + len(steps) :]
    core, first, second = place()
    copies = []
    for k, (shift, (begin, end), added) in enumerate(steps):
        half = core if added else 1 - core
        at = lax.rem((first if added else second) + shift, RING)
        for zh in range(begin, end):
            target, sem = held.at[k, zh - begin], sems.at[k, zh - begin]
            along_x = pltpu.make_async_copy(grads.at[zh, half, at], target, sem)
            along_y = pltpu.make_async_copy(grads.at[zh, half, :, at], target, sem)
            pl.when(half == 0)(along_x.start)
            pl.when(half != 0)(along_y.start)
            copies.append(along_x)
    copies = iter(copies)
    for k, (_, (begin, end), added) in enumerate(steps):
        source = received.pop(0) if added else None
        for zh in range(end - begin):
            next(copies).wait()
            for other in range(RING):
                value = held[k, zh, other]
                if added:
                    value += source[zh, other].astype(F32)
                outs[k][zh, other] = value.astype(outs[k].dtype)


VMEM = pl.BlockSpec(memory_space=pltpu.VMEM)
PARAMS = pltpu.CompilerParams(vmem_limit_bytes=10 * 1024 * 1024)
COST = pl.CostEstimate(flops=0, bytes_accessed=0, transcendentals=0)


def run_steps(grads, steps, received=(), dtype=BF16):
    rows, lanes = grads.shape[-2:]
    longest = max(end - begin for _, (begin, end), _ in steps)
    return pl.pallas_call(
        functools.partial(steps_kernel, steps),
        out_shape=[pltpu.VMEM((end - begin, RING, rows, lanes), dtype) for _, (begin, end), _ in steps],
        in_specs=[pl.BlockSpec(memory_space=pltpu.HBM)] + [VMEM] * len(received),
        out_specs=[VMEM] * len(steps),
        scratch_shapes=[
            pltpu.VMEM((len(steps), longest, RING, rows, lanes), F32),
            pltpu.SemaphoreType.DMA((len(steps), longest)),
        ],
        compiler_params=PARAMS,
        cost_estimate=COST,
    )(pltpu.with_memory_space_constraint(grads, pltpu.HBM), *received)


def sum_kernel(parts, own, *refs):
    arrived, outs = refs[: len(parts)], refs[len(parts) :]
    second = place()[2]
    for shift, out in enumerate(outs):
        other = lax.rem(second + shift, RING)
        for zh in range(ZH):
            value = own[zh, other]
            for (begin, end), part in zip(parts, arrived):
                if begin <= zh < end:
                    value += part[zh - begin, other].astype(F32)
            out[zh] = value.astype(out.dtype)


def run_sum(own, parts, arrived):
    rows, lanes = own.shape[-2:]
    return pl.pallas_call(
        functools.partial(sum_kernel, parts),
        out_shape=[pltpu.VMEM((ZH, rows, lanes), BF16 if shift else F32) for shift in range(RING)],
        in_specs=[VMEM] * (1 + len(arrived)),
        out_specs=[VMEM] * RING,
        compiler_params=PARAMS,
        cost_estimate=COST,
    )(own, *[pltpu.with_memory_space_constraint(part, pltpu.VMEM) for part in arrived])


def on_device(grads):
    blocks = grads.shape[1] // (ZH * CORE * X * Y * ZL * QB)
    grads = grads.reshape(ZH, CORE, X, Y, ZL * blocks, QB)
    whole, low, high = (0, ZH), (0, ZH // 2), (ZH // 2, ZH)
    order = (
        ((2, whole, False),),
        ((1, whole, False), (3, whole, False), (0, whole, False)),
        ((2, whole, True),),
        ((1, whole, True),),
        ((3, whole, True),),
        ((0, whole, True),),
    )
    crossed, arrived, own = {}, {}, None
    for steps in order:
        received = [crossed[shift, part] for shift, part, added in steps if added]
        outs = run_steps(grads, steps, received, BF16 if steps[0] != (0, whole, True) else F32)
        grads = lax.optimization_barrier((grads, *outs))[0]
        for (shift, part, added), out in zip(steps, outs):
            if not added:
                crossed[shift, part] = to_other_core(out)
            elif shift:
                arrived[shift, part] = along(out, shift, True)
            else:
                own = out

    pieces = run_sum(own, [part for _, part in arrived], list(arrived.values()))
    summed = pieces[0]
    for shift in (2, 1, 3):
        summed += along(pieces[shift], shift, False).astype(F32)
    pieces = summed.astype(BF16).reshape(ZH * ZL, blocks, QB)
    pieces = lax.all_to_all(pieces, AXES, 0, 0, axis_index_groups=z_groups(), tiled=True)
    return jnp.sum(pieces.astype(F32), axis=0).reshape(blocks * QB)


def solution(mesh):
    placed = (P(("node", "group"), None),)
    return jax.shard_map(
        on_device, mesh=mesh, in_specs=placed, out_specs=P(("node", "group")), check_vma=False
    )
```

```python
import functools

import jax
import jax.numpy as jnp
from jax import lax
from jax.experimental import pallas as pl
from jax.experimental.pallas import tpu as pltpu
from jax.sharding import PartitionSpec as P

QB = 128
ZH, CORE, X, Y, ZL = 4, 2, 4, 4, 2
RING = 4
AXES = ("node", "group")
BF16, F32 = jnp.bfloat16, jnp.float32
SLABS, PLAIN = 6, 4


def flat(zh, c, x, y, zl):
    return (((zh * CORE + c) * X + x) * Y + y) * ZL + zl


def permuted(values, move):
    pairs = []
    for zh in range(ZH):
        for c in range(CORE):
            for x in range(X):
                for y in range(Y):
                    for zl in range(ZL):
                        pairs.append((flat(zh, c, x, y, zl), flat(*move(zh, c, x, y, zl))))
    return lax.ppermute(values, AXES, pairs)


def to_other_core(values):
    return permuted(values, lambda zh, c, x, y, zl: (zh, 1 - c, x, y, zl))


def along(values, shift, first):
    def move(zh, c, x, y, zl):
        if (c == 0) == first:
            return zh, c, (x + shift) % X, y, zl
        return zh, c, x, (y + shift) % Y, zl

    return permuted(values, move)


def to_z_partner(values):
    def move(zh, c, x, y, zl):
        step = 1 if (zl == 0) == (c == 0) else -1
        z = (zh * ZL + zl + step) % (ZH * ZL)
        return z // ZL, c, x, y, z % ZL

    return permuted(values, move)


def z_groups():
    groups = []
    for c in range(CORE):
        for x in range(X):
            for y in range(Y):
                groups.append([flat(zh, c, x, y, zl) for zh in range(ZH) for zl in range(ZL)])
    return groups


def place():
    node, group = lax.axis_index("node"), lax.axis_index("group")
    core = lax.rem(node, CORE)
    x, y = lax.div(group, Y * ZL), lax.rem(lax.div(group, ZL), Y)
    return core, jnp.where(core == 0, x, y), jnp.where(core == 0, y, x), lax.rem(group, ZL)


PAIR, SENT, KEPT = "pair", "sent", "kept"


def shape_of(what, rows):
    if what == PAIR:
        return (ZH, X, Y, ZL, SLABS - PLAIN, rows, QB)
    if what in (SENT, KEPT):
        return (ZH, X, Y, ZL, rows, QB)
    return (ZH, RING, ZL, PLAIN, rows, QB)


def steps_kernel(steps, grads, *refs):
    n_received = sum(added for _, added in steps)
    received, outs = list(refs[:n_received]), refs[n_received : n_received + len(steps)]
    helds, sems = refs[n_received + len(steps) : -1], refs[-1]
    core, first, second, zl = place()
    copies = []
    for k, (what, added) in enumerate(steps):
        half = core if added else 1 - core
        for zh in range(ZH):
            target, sem = helds[k].at[zh], sems.at[k, zh]
            if what == PAIR:
                copy = pltpu.make_async_copy(grads.at[zh, half, :, :, :, pl.ds(PLAIN, SLABS - PLAIN)], target, sem)
                copy.start()
            elif what in (SENT, KEPT):
                slab = PLAIN + (1 - zl if what == SENT else zl)
                copy = pltpu.make_async_copy(grads.at[zh, half, :, :, :, slab], target, sem)
                copy.start()
            else:
                at = lax.rem((first if added else second) + what, RING)
                copy = pltpu.make_async_copy(grads.at[zh, half, at, :, :, pl.ds(0, PLAIN)], target, sem)
                along_y = pltpu.make_async_copy(grads.at[zh, half, :, at, :, pl.ds(0, PLAIN)], target, sem)
                pl.when(half == 0)(copy.start)
                pl.when(half != 0)(along_y.start)
            copies.append(copy)
    copies = iter(copies)
    for k, (what, added) in enumerate(steps):
        source = received.pop(0) if added else None
        for zh in range(ZH):
            next(copies).wait()
            value = helds[k][zh]
            if added and what in (SENT, KEPT):
                value += source[zh, :, :, :, 1 - zl if what == SENT else zl].astype(F32)
            elif added:
                value += source[zh].astype(F32)
            outs[k][zh] = value.astype(outs[k].dtype)


VMEM = pl.BlockSpec(memory_space=pltpu.VMEM)
PARAMS = pltpu.CompilerParams(vmem_limit_bytes=10 * 1024 * 1024)
COST = pl.CostEstimate(flops=0, bytes_accessed=0, transcendentals=0)


def in_vmem(values):
    return pltpu.with_memory_space_constraint(values, pltpu.VMEM)


def run_steps(grads, steps, received):
    rows = grads.shape[-2]
    shapes = [shape_of(what, rows) for what, _ in steps]
    types = [F32 if added and what in (0, KEPT) else BF16 for what, added in steps]
    return pl.pallas_call(
        functools.partial(steps_kernel, steps),
        out_shape=[pltpu.VMEM(shape, dtype) for shape, dtype in zip(shapes, types)],
        in_specs=[pl.BlockSpec(memory_space=pltpu.HBM)] + [VMEM] * len(received),
        out_specs=[VMEM] * len(steps),
        scratch_shapes=[pltpu.VMEM(shape, F32) for shape in shapes] + [pltpu.SemaphoreType.DMA((len(steps), ZH))],
        compiler_params=PARAMS,
        cost_estimate=COST,
    )(pltpu.with_memory_space_constraint(grads, pltpu.HBM), *received)


def paired_kernel(kept, arrived, *outs):
    core, first, _, _ = place()
    for shift, out in enumerate(outs):
        at = lax.rem(first + shift, RING)
        for zh in range(ZH):
            for other in range(RING):
                x, y = jnp.where(core == 0, at, other), jnp.where(core == 0, other, at)
                out[zh, other] = (kept[zh, x, y] + arrived[zh, x, y].astype(F32)).astype(out.dtype)


def run_paired(kept, arrived):
    rows = kept.shape[-2]
    return pl.pallas_call(
        paired_kernel,
        out_shape=[pltpu.VMEM((ZH, RING, ZL, rows, QB), BF16 if shift else F32) for shift in range(RING)],
        in_specs=[VMEM] * 2,
        out_specs=[VMEM] * RING,
        compiler_params=PARAMS,
        cost_estimate=COST,
    )(kept, in_vmem(arrived))


def plain_kernel(own, p1, p2, p3, out):
    for zh in range(ZH):
        out[zh] = own[zh] + p1[zh].astype(F32) + p2[zh].astype(F32) + p3[zh].astype(F32)


def run_plain(own, arrived):
    return pl.pallas_call(
        plain_kernel,
        out_shape=pltpu.VMEM(own.shape, F32),
        in_specs=[VMEM] * 4,
        out_specs=VMEM,
        compiler_params=PARAMS,
        cost_estimate=COST,
    )(own, *map(in_vmem, arrived))


def pieces_kernel(plain, own, p1, p2, p3, *outs):
    second = place()[2]
    for shift, out in enumerate(outs):
        other = lax.rem(second + shift, RING)
        for zh in range(ZH):
            paired = own[zh, other] + p1[zh, other].astype(F32) + p2[zh, other].astype(F32) + p3[zh, other].astype(F32)
            out[zh, :, 0:PLAIN] = plain[zh, other].astype(out.dtype)
            out[zh, :, PLAIN] = paired.astype(out.dtype)


def run_pieces(plain, own, arrived):
    rows = own.shape[-2]
    return pl.pallas_call(
        pieces_kernel,
        out_shape=[pltpu.VMEM((ZH, ZL, PLAIN + 1, rows, QB), BF16 if shift else F32) for shift in range(RING)],
        in_specs=[VMEM] * 5,
        out_specs=[VMEM] * RING,
        compiler_params=PARAMS,
        cost_estimate=COST,
    )(plain, own, *map(in_vmem, arrived))


def on_device(grads):
    rows = grads.shape[1] // (ZH * CORE * X * Y * ZL * SLABS * QB)
    grads = grads.reshape(ZH, CORE, X, Y, ZL, SLABS, rows, QB)
    order = (
        ((2, False), (PAIR, False)),
        ((1, False), (3, False), (0, False)),
        ((2, True), (SENT, True)),
        ((1, True),),
        ((3, True),),
        ((0, True), (KEPT, True)),
    )
    crossed, arrived, own = {}, {}, {}
    for steps in order:
        received = [crossed[PAIR if what in (SENT, KEPT) else what] for what, added in steps if added]
        outs = run_steps(grads, steps, received)
        grads = lax.optimization_barrier((grads, *outs))[0]
        for (what, added), out in zip(steps, outs):
            if not added:
                crossed[what] = to_other_core(out)
            elif what == SENT:
                arrived[what] = to_z_partner(out)
            elif what in (0, KEPT):
                own[what] = out
            else:
                arrived[what] = along(out, what, True)

    paired = run_paired(own[KEPT], arrived[SENT])
    paired_arrived = {shift: along(paired[shift], shift, True) for shift in (2, 1, 3)}
    plain = run_plain(own[0], [arrived[shift] for shift in (2, 1, 3)])
    pieces = run_pieces(plain, paired[0], [paired_arrived[shift] for shift in (2, 1, 3)])
    summed = pieces[0]
    for shift in (2, 1, 3):
        summed += along(pieces[shift], shift, False).astype(F32)
    pieces = summed.astype(BF16).reshape(ZH * ZL, PLAIN + 1, rows, QB)
    pieces = lax.all_to_all(pieces, AXES, 0, 0, axis_index_groups=z_groups(), tiled=True).astype(F32)
    of_plain = jnp.sum(pieces[:, :PLAIN], axis=0)
    of_paired = jnp.sum(pieces[:, PLAIN].reshape(ZH, ZL, rows, QB), axis=0)
    return jnp.concatenate([of_plain, of_paired]).reshape(SLABS * rows * QB)


def solution(mesh):
    placed = (P(("node", "group"), None),)
    return jax.shard_map(
        on_device, mesh=mesh, in_specs=placed, out_specs=P(("node", "group")), check_vma=False
    )
```

```python
import functools

import jax
import jax.numpy as jnp
from jax import lax
from jax.experimental import pallas as pl
from jax.experimental.pallas import tpu as pltpu
from jax.sharding import PartitionSpec as P

QB = 128
ZH, CORE, X, Y, ZL = 4, 2, 4, 4, 2
RING = 4
AXES = ("node", "group")
BF16, F32 = jnp.bfloat16, jnp.float32
SLABS, PLAIN = 6, 4


def flat(zh, c, x, y, zl):
    return (((zh * CORE + c) * X + x) * Y + y) * ZL + zl


def permuted(values, move):
    pairs = []
    for zh in range(ZH):
        for c in range(CORE):
            for x in range(X):
                for y in range(Y):
                    for zl in range(ZL):
                        pairs.append((flat(zh, c, x, y, zl), flat(*move(zh, c, x, y, zl))))
    return lax.ppermute(values, AXES, pairs)


def to_other_core(values):
    return permuted(values, lambda zh, c, x, y, zl: (zh, 1 - c, x, y, zl))


def along(values, shift, first):
    def move(zh, c, x, y, zl):
        if (c == 0) == first:
            return zh, c, (x + shift) % X, y, zl
        return zh, c, x, (y + shift) % Y, zl

    return permuted(values, move)


def to_z_partner(values):
    def move(zh, c, x, y, zl):
        step = 1 if (zl == 0) == (c == 0) else -1
        z = (zh * ZL + zl + step) % (ZH * ZL)
        return z // ZL, c, x, y, z % ZL

    return permuted(values, move)


def z_groups():
    groups = []
    for c in range(CORE):
        for x in range(X):
            for y in range(Y):
                groups.append([flat(zh, c, x, y, zl) for zh in range(ZH) for zl in range(ZL)])
    return groups


def place():
    node, group = lax.axis_index("node"), lax.axis_index("group")
    core = lax.rem(node, CORE)
    x, y = lax.div(group, Y * ZL), lax.rem(lax.div(group, ZL), Y)
    return core, jnp.where(core == 0, x, y), jnp.where(core == 0, y, x), lax.rem(group, ZL)


SENT, KEPT = "sent", "kept"


def shape_of(what, rows):
    if what in (SENT, KEPT):
        return (ZH, X, Y, ZL, rows, QB)
    return (ZH, RING, ZL, PLAIN, rows, QB)


def slabs_of(what):
    return X * Y * ZL if what in (SENT, KEPT) else RING * ZL * PLAIN


def fetch(grads, what, half, at, zl, zh, target, sem):
    if what in (SENT, KEPT):
        slab = PLAIN + (1 - zl if what == SENT else zl)
        copy = pltpu.make_async_copy(grads.at[zh, half, :, :, :, slab], target, sem)
        copy.start()
        return copy
    copy = pltpu.make_async_copy(grads.at[zh, half, at, :, :, pl.ds(0, PLAIN)], target, sem)
    along_y = pltpu.make_async_copy(grads.at[zh, half, :, at, :, pl.ds(0, PLAIN)], target, sem)
    pl.when(half == 0)(copy.start)
    pl.when(half != 0)(along_y.start)
    return copy


def fetch_all(grads, steps, half, first, zl, helds, sems):
    copies = []
    for k, what in enumerate(steps):
        at = first if what in (SENT, KEPT) else lax.rem(first + what, RING)
        for zh in range(ZH):
            copies.append(fetch(grads, what, half, at, zl, zh, helds[k].at[zh], sems.at[k, zh]))
    return copies


def cast_kernel(groups, grads, *refs):
    outs, helds, sems = refs[: len(groups)], refs[len(groups) : -1], refs[-1]
    core, _, second, zl = place()
    steps = [what for group in groups for what in group]
    copies = iter(fetch_all(grads, steps, 1 - core, second, zl, helds, sems))
    helds = iter(helds)
    for group, out in zip(groups, outs):
        begin = 0
        for what in group:
            held, end = next(helds), begin + slabs_of(what)
            for zh in range(ZH):
                next(copies).wait()
                out[zh, begin:end] = held[zh].reshape(end - begin, *held.shape[-2:]).astype(out.dtype)
            begin = end


def add_kernel(group, grads, received, *refs):
    outs, helds, sems = refs[: len(group)], refs[len(group) : -1], refs[-1]
    core, first, _, zl = place()
    copies = iter(fetch_all(grads, group, core, first, zl, helds, sems))
    begin = 0
    for what, out, held in zip(group, outs, helds):
        end = begin + slabs_of(what)
        for zh in range(ZH):
            next(copies).wait()
            value = held[zh] + received[zh, begin:end].reshape(held.shape[1:]).astype(F32)
            out[zh] = value.astype(out.dtype)
        begin = end


VMEM = pl.BlockSpec(memory_space=pltpu.VMEM)
PARAMS = pltpu.CompilerParams(vmem_limit_bytes=10 * 1024 * 1024)
COST = pl.CostEstimate(flops=0, bytes_accessed=0, transcendentals=0)


def in_vmem(values):
    return pltpu.with_memory_space_constraint(values, pltpu.VMEM)


def run_on_grads(kernel, grads, steps, out_shape, received=()):
    rows = grads.shape[-2]
    return pl.pallas_call(
        kernel,
        out_shape=out_shape,
        in_specs=[pl.BlockSpec(memory_space=pltpu.HBM)] + [VMEM] * len(received),
        out_specs=[VMEM] * len(out_shape),
        scratch_shapes=[pltpu.VMEM(shape_of(what, rows), F32) for what in steps]
        + [pltpu.SemaphoreType.DMA((len(steps), ZH))],
        compiler_params=PARAMS,
        cost_estimate=COST,
    )(pltpu.with_memory_space_constraint(grads, pltpu.HBM), *received)


def run_cast(grads, groups):
    rows = grads.shape[-2]
    out_shape = [pltpu.VMEM((ZH, sum(map(slabs_of, group)), rows, QB), BF16) for group in groups]
    steps = [what for group in groups for what in group]
    return run_on_grads(functools.partial(cast_kernel, groups), grads, steps, out_shape)


def run_add(grads, group, received):
    rows = grads.shape[-2]
    out_shape = [pltpu.VMEM(shape_of(what, rows), F32 if what in (0, KEPT) else BF16) for what in group]
    return run_on_grads(functools.partial(add_kernel, group), grads, group, out_shape, [received])


def paired_kernel(kept, arrived, *outs):
    core, first, _, _ = place()
    for shift, out in enumerate(outs):
        at = lax.rem(first + shift, RING)
        for zh in range(ZH):
            for other in range(RING):
                x, y = jnp.where(core == 0, at, other), jnp.where(core == 0, other, at)
                out[zh, other] = (kept[zh, x, y] + arrived[zh, x, y].astype(F32)).astype(out.dtype)


def run_paired(kept, arrived):
    rows = kept.shape[-2]
    return pl.pallas_call(
        paired_kernel,
        out_shape=[pltpu.VMEM((ZH, RING, ZL, rows, QB), BF16 if shift else F32) for shift in range(RING)],
        in_specs=[VMEM] * 2,
        out_specs=[VMEM] * RING,
        compiler_params=PARAMS,
        cost_estimate=COST,
    )(kept, in_vmem(arrived))


def plain_kernel(own, p1, p2, p3, out):
    for zh in range(ZH):
        out[zh] = own[zh] + p1[zh].astype(F32) + p2[zh].astype(F32) + p3[zh].astype(F32)


def run_plain(own, arrived):
    return pl.pallas_call(
        plain_kernel,
        out_shape=pltpu.VMEM(own.shape, F32),
        in_specs=[VMEM] * 4,
        out_specs=VMEM,
        compiler_params=PARAMS,
        cost_estimate=COST,
    )(own, *map(in_vmem, arrived))


def pieces_kernel(plain, own, p1, p2, p3, *outs):
    second = place()[2]
    for shift, out in enumerate(outs):
        other = lax.rem(second + shift, RING)
        for zh in range(ZH):
            paired = own[zh, other] + p1[zh, other].astype(F32) + p2[zh, other].astype(F32) + p3[zh, other].astype(F32)
            out[zh, :, 0:PLAIN] = plain[zh, other].astype(out.dtype)
            out[zh, :, PLAIN] = paired.astype(out.dtype)


def run_pieces(plain, own, arrived):
    rows = own.shape[-2]
    return pl.pallas_call(
        pieces_kernel,
        out_shape=[pltpu.VMEM((ZH, ZL, PLAIN + 1, rows, QB), BF16 if shift else F32) for shift in range(RING)],
        in_specs=[VMEM] * 5,
        out_specs=[VMEM] * RING,
        compiler_params=PARAMS,
        cost_estimate=COST,
    )(plain, own, *map(in_vmem, arrived))


def on_device(grads):
    rows = grads.shape[1] // (ZH * CORE * X * Y * ZL * SLABS * QB)
    grads = grads.reshape(ZH, CORE, X, Y, ZL, SLABS, rows, QB)
    groups = ((2, SENT), (1, 3), (0, KEPT))
    crossed = []
    for some in (groups[:1], groups[1:]):
        outs = run_cast(grads, some)
        grads = lax.optimization_barrier((grads, *outs))[0]
        crossed += [to_other_core(out) for out in outs]
    arrived, own = {}, {}
    for group, received in zip(groups, crossed):
        outs = run_add(grads, group, received)
        grads = lax.optimization_barrier((grads, *outs))[0]
        for what, out in zip(group, outs):
            if what == SENT:
                arrived[what] = to_z_partner(out)
            elif what in (0, KEPT):
                own[what] = out
            else:
                arrived[what] = along(out, what, True)

    paired = run_paired(own[KEPT], arrived[SENT])
    paired_arrived = {shift: along(paired[shift], shift, True) for shift in (2, 1, 3)}
    plain = run_plain(own[0], [arrived[shift] for shift in (2, 1, 3)])
    pieces = run_pieces(plain, paired[0], [paired_arrived[shift] for shift in (2, 1, 3)])
    summed = pieces[0]
    for shift in (2, 1, 3):
        summed += along(pieces[shift], shift, False).astype(F32)
    pieces = summed.astype(BF16).reshape(ZH * ZL, PLAIN + 1, rows, QB)
    pieces = lax.all_to_all(pieces, AXES, 0, 0, axis_index_groups=z_groups(), tiled=True).astype(F32)
    of_plain = jnp.sum(pieces[:, :PLAIN], axis=0)
    of_paired = jnp.sum(pieces[:, PLAIN].reshape(ZH, ZL, rows, QB), axis=0)
    return jnp.concatenate([of_plain, of_paired]).reshape(SLABS * rows * QB)


def solution(mesh):
    placed = (P(("node", "group"), None),)
    return jax.shard_map(
        on_device, mesh=mesh, in_specs=placed, out_specs=P(("node", "group")), check_vma=False
    )
```

```python
import functools

import jax
import jax.numpy as jnp
from jax import lax
from jax.experimental import pallas as pl
from jax.experimental.pallas import tpu as pltpu
from jax.sharding import PartitionSpec as P

QB = 128
ZH, CORE, X, Y, ZL = 4, 2, 4, 4, 2
RING = 4
AXES = ("node", "group")
BF16, F32 = jnp.bfloat16, jnp.float32
SLABS, PLAIN = 6, 4


def flat(zh, c, x, y, zl):
    return (((zh * CORE + c) * X + x) * Y + y) * ZL + zl


def permuted(values, move):
    pairs = []
    for zh in range(ZH):
        for c in range(CORE):
            for x in range(X):
                for y in range(Y):
                    for zl in range(ZL):
                        pairs.append((flat(zh, c, x, y, zl), flat(*move(zh, c, x, y, zl))))
    return lax.ppermute(values, AXES, pairs)


def to_other_core(values):
    return permuted(values, lambda zh, c, x, y, zl: (zh, 1 - c, x, y, zl))


def along(values, shift, first):
    def move(zh, c, x, y, zl):
        if (c == 0) == first:
            return zh, c, (x + shift) % X, y, zl
        return zh, c, x, (y + shift) % Y, zl

    return permuted(values, move)


def to_z_partner(values):
    def move(zh, c, x, y, zl):
        step = 1 if (zl == 0) == (c == 0) else -1
        z = (zh * ZL + zl + step) % (ZH * ZL)
        return z // ZL, c, x, y, z % ZL

    return permuted(values, move)


def z_groups():
    groups = []
    for c in range(CORE):
        for x in range(X):
            for y in range(Y):
                groups.append([flat(zh, c, x, y, zl) for zh in range(ZH) for zl in range(ZL)])
    return groups


def place():
    node, group = lax.axis_index("node"), lax.axis_index("group")
    core = lax.rem(node, CORE)
    x, y = lax.div(group, Y * ZL), lax.rem(lax.div(group, ZL), Y)
    return core, jnp.where(core == 0, x, y), jnp.where(core == 0, y, x), lax.rem(group, ZL)


SENT, KEPT = "sent", "kept"


def shape_of(what, rows):
    if what in (SENT, KEPT):
        return (ZH, X, Y, ZL, rows, QB)
    return (ZH, RING, ZL, PLAIN, rows, QB)


def slabs_of(what):
    return X * Y * ZL if what in (SENT, KEPT) else RING * ZL * PLAIN


def fetch(grads, what, half, at, zl, zh, target, sem):
    if what in (SENT, KEPT):
        slab = PLAIN + (1 - zl if what == SENT else zl)
        copy = pltpu.make_async_copy(grads.at[zh, half, :, :, :, slab], target, sem)
        copy.start()
        return copy
    copy = pltpu.make_async_copy(grads.at[zh, half, at, :, :, pl.ds(0, PLAIN)], target, sem)
    along_y = pltpu.make_async_copy(grads.at[zh, half, :, at, :, pl.ds(0, PLAIN)], target, sem)
    pl.when(half == 0)(copy.start)
    pl.when(half != 0)(along_y.start)
    return copy


def fetch_all(grads, steps, half, first, zl, helds, sems, skip=0):
    copies = []
    for k, what in enumerate(steps):
        at = first if what in (SENT, KEPT) else lax.rem(first + what, RING)
        for zh in range(ZH):
            copies.append(fetch(grads, what, half, at, zl, zh, helds[k].at[zh], sems.at[skip + k, zh]))
    return copies


def cast_kernel(groups, kept, grads, *refs):
    outs, refs = refs[: len(groups)], refs[len(groups) :]
    keeps, helds, sems = refs[: len(kept)], refs[len(kept) : -1], refs[-1]
    core, first, second, zl = place()
    steps = [what for group in groups for what in group]
    copies = iter(
        fetch_all(grads, steps, 1 - core, second, zl, helds, sems)
        + fetch_all(grads, kept, core, first, zl, keeps, sems, len(steps))
    )
    helds = iter(helds)
    for group, out in zip(groups, outs):
        begin = 0
        for what in group:
            held, end = next(helds), begin + slabs_of(what)
            for zh in range(ZH):
                next(copies).wait()
                out[zh, begin:end] = held[zh].reshape(end - begin, *held.shape[-2:]).astype(out.dtype)
            begin = end
    for copy in copies:
        copy.wait()


def add_kept_kernel(group, received, *refs):
    keeps, outs = refs[: len(group)], refs[len(group) :]
    begin = 0
    for what, kept, out in zip(group, keeps, outs):
        end = begin + slabs_of(what)
        for zh in range(ZH):
            out[zh] = (kept[zh] + received[zh, begin:end].reshape(kept.shape[1:]).astype(F32)).astype(out.dtype)
        begin = end


def add_kernel(group, grads, received, *refs):
    outs, helds, sems = refs[: len(group)], refs[len(group) : -1], refs[-1]
    core, first, _, zl = place()
    copies = iter(fetch_all(grads, group, core, first, zl, helds, sems))
    begin = 0
    for what, out, held in zip(group, outs, helds):
        end = begin + slabs_of(what)
        for zh in range(ZH):
            next(copies).wait()
            value = held[zh] + received[zh, begin:end].reshape(held.shape[1:]).astype(F32)
            out[zh] = value.astype(out.dtype)
        begin = end


VMEM = pl.BlockSpec(memory_space=pltpu.VMEM)
PARAMS = pltpu.CompilerParams(vmem_limit_bytes=10 * 1024 * 1024)
COST = pl.CostEstimate(flops=0, bytes_accessed=0, transcendentals=0)


def in_vmem(values):
    return pltpu.with_memory_space_constraint(values, pltpu.VMEM)


def run_on_grads(kernel, grads, steps, out_shape, received=(), kept=()):
    rows = grads.shape[-2]
    return pl.pallas_call(
        kernel,
        out_shape=out_shape,
        in_specs=[pl.BlockSpec(memory_space=pltpu.HBM)] + [VMEM] * len(received),
        out_specs=[VMEM] * len(out_shape),
        scratch_shapes=[pltpu.VMEM(shape_of(what, rows), F32) for what in steps]
        + [pltpu.SemaphoreType.DMA((len(steps) + len(kept), ZH))],
        compiler_params=PARAMS,
        cost_estimate=COST,
    )(pltpu.with_memory_space_constraint(grads, pltpu.HBM), *received)


def run_cast(grads, groups, kept):
    rows = grads.shape[-2]
    out_shape = [pltpu.VMEM((ZH, sum(map(slabs_of, group)), rows, QB), BF16) for group in groups]
    out_shape += [pltpu.VMEM(shape_of(what, rows), F32) for what in kept]
    steps = [what for group in groups for what in group]
    return run_on_grads(functools.partial(cast_kernel, groups, kept), grads, steps, out_shape, kept=kept)


def add_shape(group, rows):
    return [pltpu.VMEM(shape_of(what, rows), F32 if what in (0, KEPT) else BF16) for what in group]


def run_add(grads, group, received):
    return run_on_grads(functools.partial(add_kernel, group), grads, group, add_shape(group, grads.shape[-2]), [received])


def run_add_kept(group, received, keeps):
    return pl.pallas_call(
        functools.partial(add_kept_kernel, group),
        out_shape=add_shape(group, received.shape[-2]),
        in_specs=[VMEM] * (1 + len(keeps)),
        out_specs=[VMEM] * len(group),
        compiler_params=PARAMS,
        cost_estimate=COST,
    )(received, *keeps)


def paired_kernel(kept, arrived, *outs):
    core, first, _, _ = place()
    for shift, out in enumerate(outs):
        at = lax.rem(first + shift, RING)
        for zh in range(ZH):
            for other in range(RING):
                x, y = jnp.where(core == 0, at, other), jnp.where(core == 0, other, at)
                out[zh, other] = (kept[zh, x, y] + arrived[zh, x, y].astype(F32)).astype(out.dtype)


def run_paired(kept, arrived):
    rows = kept.shape[-2]
    return pl.pallas_call(
        paired_kernel,
        out_shape=[pltpu.VMEM((ZH, RING, ZL, rows, QB), BF16 if shift else F32) for shift in range(RING)],
        in_specs=[VMEM] * 2,
        out_specs=[VMEM] * RING,
        compiler_params=PARAMS,
        cost_estimate=COST,
    )(kept, in_vmem(arrived))


def plain_kernel(own, p1, p2, p3, out):
    for zh in range(ZH):
        out[zh] = own[zh] + p1[zh].astype(F32) + p2[zh].astype(F32) + p3[zh].astype(F32)


def run_plain(own, arrived):
    return pl.pallas_call(
        plain_kernel,
        out_shape=pltpu.VMEM(own.shape, F32),
        in_specs=[VMEM] * 4,
        out_specs=VMEM,
        compiler_params=PARAMS,
        cost_estimate=COST,
    )(own, *map(in_vmem, arrived))


def pieces_kernel(plain, own, p1, p2, p3, *outs):
    second = place()[2]
    for shift, out in enumerate(outs):
        other = lax.rem(second + shift, RING)
        for zh in range(ZH):
            paired = own[zh, other] + p1[zh, other].astype(F32) + p2[zh, other].astype(F32) + p3[zh, other].astype(F32)
            out[zh, :, 0:PLAIN] = plain[zh, other].astype(out.dtype)
            out[zh, :, PLAIN] = paired.astype(out.dtype)


def run_pieces(plain, own, arrived):
    rows = own.shape[-2]
    return pl.pallas_call(
        pieces_kernel,
        out_shape=[pltpu.VMEM((ZH, ZL, PLAIN + 1, rows, QB), BF16 if shift else F32) for shift in range(RING)],
        in_specs=[VMEM] * 5,
        out_specs=[VMEM] * RING,
        compiler_params=PARAMS,
        cost_estimate=COST,
    )(plain, own, *map(in_vmem, arrived))


def on_device(grads):
    rows = grads.shape[1] // (ZH * CORE * X * Y * ZL * SLABS * QB)
    grads = grads.reshape(ZH, CORE, X, Y, ZL, SLABS, rows, QB)
    groups = ((2, SENT), (1, 3), (0, KEPT))
    outs = run_cast(grads, groups[:1], ())
    grads = lax.optimization_barrier((grads, *outs))[0]
    crossed = [to_other_core(out) for out in outs]
    outs = run_cast(grads, groups[1:], groups[0])
    grads = lax.optimization_barrier((grads, *outs))[0]
    crossed += [to_other_core(out) for out in outs[:2]]
    arrived, own = {}, {}
    for group, received in zip(groups, crossed):
        summed = run_add(grads, group, received) if group != groups[0] else run_add_kept(group, received, outs[2:])
        grads = lax.optimization_barrier((grads, *summed))[0]
        for what, out in zip(group, summed):
            if what == SENT:
                arrived[what] = to_z_partner(out)
            elif what in (0, KEPT):
                own[what] = out
            else:
                arrived[what] = along(out, what, True)

    paired = run_paired(own[KEPT], arrived[SENT])
    paired_arrived = {shift: along(paired[shift], shift, True) for shift in (2, 1, 3)}
    plain = run_plain(own[0], [arrived[shift] for shift in (2, 1, 3)])
    pieces = run_pieces(plain, paired[0], [paired_arrived[shift] for shift in (2, 1, 3)])
    summed = pieces[0]
    for shift in (2, 1, 3):
        summed += along(pieces[shift], shift, False).astype(F32)
    pieces = summed.astype(BF16).reshape(ZH * ZL, PLAIN + 1, rows, QB)
    pieces = lax.all_to_all(pieces, AXES, 0, 0, axis_index_groups=z_groups(), tiled=True).astype(F32)
    of_plain = jnp.sum(pieces[:, :PLAIN], axis=0)
    of_paired = jnp.sum(pieces[:, PLAIN].reshape(ZH, ZL, rows, QB), axis=0)
    return jnp.concatenate([of_plain, of_paired]).reshape(SLABS * rows * QB)


def solution(mesh):
    placed = (P(("node", "group"), None),)
    return jax.shard_map(
        on_device, mesh=mesh, in_specs=placed, out_specs=P(("node", "group")), check_vma=False
    )
```

```python
import functools

import jax
import jax.numpy as jnp
from jax import lax
from jax.experimental import pallas as pl
from jax.experimental.pallas import tpu as pltpu
from jax.sharding import PartitionSpec as P

QB = 128
ZH, CORE, X, Y, ZL = 4, 2, 4, 4, 2
RING = 4
AXES = ("node", "group")
BF16, F32 = jnp.bfloat16, jnp.float32
SLABS, PLAIN = 6, 4


def flat(zh, c, x, y, zl):
    return (((zh * CORE + c) * X + x) * Y + y) * ZL + zl


def permuted(values, move):
    pairs = []
    for zh in range(ZH):
        for c in range(CORE):
            for x in range(X):
                for y in range(Y):
                    for zl in range(ZL):
                        pairs.append((flat(zh, c, x, y, zl), flat(*move(zh, c, x, y, zl))))
    return lax.ppermute(values, AXES, pairs)


def to_other_core(values):
    return permuted(values, lambda zh, c, x, y, zl: (zh, 1 - c, x, y, zl))


def along(values, shift, first):
    def move(zh, c, x, y, zl):
        if (c == 0) == first:
            return zh, c, (x + shift) % X, y, zl
        return zh, c, x, (y + shift) % Y, zl

    return permuted(values, move)


def to_z_partner(values):
    def move(zh, c, x, y, zl):
        step = 1 if (zl == 0) == (c == 0) else -1
        z = (zh * ZL + zl + step) % (ZH * ZL)
        return z // ZL, c, x, y, z % ZL

    return permuted(values, move)


def z_groups():
    groups = []
    for c in range(CORE):
        for x in range(X):
            for y in range(Y):
                groups.append([flat(zh, c, x, y, zl) for zh in range(ZH) for zl in range(ZL)])
    return groups


def place():
    node, group = lax.axis_index("node"), lax.axis_index("group")
    core = lax.rem(node, CORE)
    x, y = lax.div(group, Y * ZL), lax.rem(lax.div(group, ZL), Y)
    return core, jnp.where(core == 0, x, y), jnp.where(core == 0, y, x), lax.rem(group, ZL)


SENT, KEPT = "sent", "kept"


def shape_of(what, rows):
    if what in (SENT, KEPT):
        return (ZH, X, Y, ZL, rows, QB)
    return (ZH, RING, ZL, PLAIN, rows, QB)


def slabs_of(what):
    return X * Y * ZL if what in (SENT, KEPT) else RING * ZL * PLAIN


def fetch(grads, what, half, at, zl, zh, target, sem):
    if what in (SENT, KEPT):
        slab = PLAIN + (1 - zl if what == SENT else zl)
        copy = pltpu.make_async_copy(grads.at[zh, half, :, :, :, slab], target, sem)
        copy.start()
        return copy
    copy = pltpu.make_async_copy(grads.at[zh, half, at, :, :, pl.ds(0, PLAIN)], target, sem)
    along_y = pltpu.make_async_copy(grads.at[zh, half, :, at, :, pl.ds(0, PLAIN)], target, sem)
    pl.when(half == 0)(copy.start)
    pl.when(half != 0)(along_y.start)
    return copy


def fetch_all(grads, steps, half, first, zl, helds, sems, skip=0):
    copies = []
    for k, what in enumerate(steps):
        at = first if what in (SENT, KEPT) else lax.rem(first + what, RING)
        for zh in range(ZH):
            copies.append(fetch(grads, what, half, at, zl, zh, helds[k].at[zh], sems.at[skip + k, zh]))
    return copies


def cast_kernel(groups, kept, grads, *refs):
    outs, refs = refs[: len(groups)], refs[len(groups) :]
    keeps, helds, sems = refs[: len(kept)], refs[len(kept) : -1], refs[-1]
    core, first, second, zl = place()
    steps = [what for group in groups for what in group]
    copies = iter(
        fetch_all(grads, steps, 1 - core, second, zl, helds, sems)
        + fetch_all(grads, kept, core, first, zl, keeps, sems, len(steps))
    )
    helds = iter(helds)
    for group, out in zip(groups, outs):
        begin = 0
        for what in group:
            held, end = next(helds), begin + slabs_of(what)
            for zh in range(ZH):
                next(copies).wait()
                out[zh, begin:end] = held[zh].reshape(end - begin, *held.shape[-2:]).astype(out.dtype)
            begin = end
    for copy in copies:
        copy.wait()


def add_kept_kernel(group, received, *refs):
    keeps, outs = refs[: len(group)], refs[len(group) :]
    begin = 0
    for what, kept, out in zip(group, keeps, outs):
        end = begin + slabs_of(what)
        for zh in range(ZH):
            out[zh] = (kept[zh] + received[zh, begin:end].reshape(kept.shape[1:]).astype(F32)).astype(out.dtype)
        begin = end


def add_kernel(group, grads, received, *refs):
    outs, helds, sems = refs[: len(group)], refs[len(group) : -1], refs[-1]
    core, first, _, zl = place()
    copies = iter(fetch_all(grads, group, core, first, zl, helds, sems))
    begin = 0
    for what, out, held in zip(group, outs, helds):
        end = begin + slabs_of(what)
        for zh in range(ZH):
            next(copies).wait()
            value = held[zh] + received[zh, begin:end].reshape(held.shape[1:]).astype(F32)
            out[zh] = value.astype(out.dtype)
        begin = end


VMEM = pl.BlockSpec(memory_space=pltpu.VMEM)
PARAMS = pltpu.CompilerParams(vmem_limit_bytes=10 * 1024 * 1024)
COST = pl.CostEstimate(flops=0, bytes_accessed=0, transcendentals=0)


def in_vmem(values):
    return pltpu.with_memory_space_constraint(values, pltpu.VMEM)


def run_on_grads(kernel, grads, steps, out_shape, received=(), kept=()):
    rows = grads.shape[-2]
    return pl.pallas_call(
        kernel,
        out_shape=out_shape,
        in_specs=[pl.BlockSpec(memory_space=pltpu.HBM)] + [VMEM] * len(received),
        out_specs=[VMEM] * len(out_shape),
        scratch_shapes=[pltpu.VMEM(shape_of(what, rows), F32) for what in steps]
        + [pltpu.SemaphoreType.DMA((len(steps) + len(kept), ZH))],
        compiler_params=PARAMS,
        cost_estimate=COST,
    )(pltpu.with_memory_space_constraint(grads, pltpu.HBM), *received)


def run_cast(grads, groups, kept):
    rows = grads.shape[-2]
    out_shape = [pltpu.VMEM((ZH, sum(map(slabs_of, group)), rows, QB), BF16) for group in groups]
    out_shape += [pltpu.VMEM(shape_of(what, rows), F32) for what in kept]
    steps = [what for group in groups for what in group]
    return run_on_grads(functools.partial(cast_kernel, groups, kept), grads, steps, out_shape, kept=kept)


def add_shape(group, rows):
    return [pltpu.VMEM(shape_of(what, rows), F32 if what in (0, KEPT) else BF16) for what in group]


def run_add(grads, group, received):
    return run_on_grads(functools.partial(add_kernel, group), grads, group, add_shape(group, grads.shape[-2]), [received])


def run_add_kept(group, received, keeps):
    return pl.pallas_call(
        functools.partial(add_kept_kernel, group),
        out_shape=add_shape(group, received.shape[-2]),
        in_specs=[VMEM] * (1 + len(keeps)),
        out_specs=[VMEM] * len(group),
        compiler_params=PARAMS,
        cost_estimate=COST,
    )(received, *keeps)


def paired_kernel(kept, arrived, *outs):
    core, first, _, _ = place()
    for shift, out in enumerate(outs):
        at = lax.rem(first + shift, RING)
        for zh in range(ZH):
            for other in range(RING):
                x, y = jnp.where(core == 0, at, other), jnp.where(core == 0, other, at)
                out[zh, other] = (kept[zh, x, y] + arrived[zh, x, y].astype(F32)).astype(out.dtype)


def run_paired(kept, arrived):
    rows = kept.shape[-2]
    return pl.pallas_call(
        paired_kernel,
        out_shape=[pltpu.VMEM((ZH, RING, ZL, rows, QB), BF16 if shift else F32) for shift in range(RING)],
        in_specs=[VMEM] * 2,
        out_specs=[VMEM] * RING,
        compiler_params=PARAMS,
        cost_estimate=COST,
    )(kept, in_vmem(arrived))


def plain_kernel(own, p1, p2, p3, out):
    for zh in range(ZH):
        out[zh] = own[zh] + p1[zh].astype(F32) + p2[zh].astype(F32) + p3[zh].astype(F32)


def run_plain(own, arrived):
    return pl.pallas_call(
        plain_kernel,
        out_shape=pltpu.VMEM(own.shape, F32),
        in_specs=[VMEM] * 4,
        out_specs=VMEM,
        compiler_params=PARAMS,
        cost_estimate=COST,
    )(own, *map(in_vmem, arrived))


def pieces_kernel(plain, own, p1, p2, p3, *outs):
    second = place()[2]
    for shift, out in enumerate(outs):
        other = lax.rem(second + shift, RING)
        for zh in range(ZH):
            paired = own[zh, other] + p1[zh, other].astype(F32) + p2[zh, other].astype(F32) + p3[zh, other].astype(F32)
            out[zh, :, 0:PLAIN] = plain[zh, other].astype(out.dtype)
            out[zh, :, PLAIN] = paired.astype(out.dtype)


def run_pieces(plain, own, arrived):
    rows = own.shape[-2]
    return pl.pallas_call(
        pieces_kernel,
        out_shape=[pltpu.VMEM((ZH, ZL, PLAIN + 1, rows, QB), BF16 if shift else F32) for shift in range(RING)],
        in_specs=[VMEM] * 5,
        out_specs=[VMEM] * RING,
        compiler_params=PARAMS,
        cost_estimate=COST,
    )(plain, own, *map(in_vmem, arrived))


def on_device(grads):
    rows = grads.shape[1] // (ZH * CORE * X * Y * ZL * SLABS * QB)
    grads = grads.reshape(ZH, CORE, X, Y, ZL, SLABS, rows, QB)
    groups = ((2, SENT), (1, 3), (0, KEPT))
    outs = run_cast(grads, groups[:1], ())
    grads = lax.optimization_barrier((grads, *outs))[0]
    crossed = [to_other_core(out) for out in outs]
    outs = run_cast(grads, groups[1:], groups[0])
    grads = lax.optimization_barrier((grads, *outs))[0]
    crossed += [to_other_core(out) for out in outs[:2]]
    arrived, own = {}, {}
    for group, received in zip(groups, crossed):
        summed = run_add(grads, group, received) if group != groups[0] else run_add_kept(group, received, outs[2:])
        grads = lax.optimization_barrier((grads, *summed))[0]
        for what, out in zip(group, summed):
            if what == SENT:
                arrived[what] = to_z_partner(out)
            elif what in (0, KEPT):
                own[what] = out
            else:
                arrived[what] = along(out, what, True)

    paired = run_paired(own[KEPT], arrived[SENT])
    paired_arrived = {shift: along(paired[shift], shift, True) for shift in (1, 3, 2)}
    plain = run_plain(own[0], [arrived[shift] for shift in (2, 1, 3)])
    pieces = run_pieces(plain, paired[0], [paired_arrived[shift] for shift in (2, 1, 3)])
    summed = pieces[0]
    for shift in (2, 1, 3):
        summed += along(pieces[shift], shift, False).astype(F32)
    pieces = summed.astype(BF16).reshape(ZH * ZL, PLAIN + 1, rows, QB)
    pieces = lax.all_to_all(pieces, AXES, 0, 0, axis_index_groups=z_groups(), tiled=True).astype(F32)
    of_plain = jnp.sum(pieces[:, :PLAIN], axis=0)
    of_paired = jnp.sum(pieces[:, PLAIN].reshape(ZH, ZL, rows, QB), axis=0)
    return jnp.concatenate([of_plain, of_paired]).reshape(SLABS * rows * QB)


def solution(mesh):
    placed = (P(("node", "group"), None),)
    return jax.shard_map(
        on_device, mesh=mesh, in_specs=placed, out_specs=P(("node", "group")), check_vma=False
    )
```

```python
import functools

import jax
import jax.numpy as jnp
from jax import lax
from jax.experimental import pallas as pl
from jax.experimental.pallas import tpu as pltpu
from jax.sharding import PartitionSpec as P

QB = 128
ZH, CORE, X, Y, ZL = 4, 2, 4, 4, 2
RING = 4
AXES = ("node", "group")
BF16, F32 = jnp.bfloat16, jnp.float32
SLABS, PLAIN = 6, 4


def flat(zh, c, x, y, zl):
    return (((zh * CORE + c) * X + x) * Y + y) * ZL + zl


def permuted(values, move):
    pairs = []
    for zh in range(ZH):
        for c in range(CORE):
            for x in range(X):
                for y in range(Y):
                    for zl in range(ZL):
                        pairs.append((flat(zh, c, x, y, zl), flat(*move(zh, c, x, y, zl))))
    return lax.ppermute(values, AXES, pairs)


def to_other_core(values):
    return permuted(values, lambda zh, c, x, y, zl: (zh, 1 - c, x, y, zl))


def along(values, shift, first):
    def move(zh, c, x, y, zl):
        if (c == 0) == first:
            return zh, c, (x + shift) % X, y, zl
        return zh, c, x, (y + shift) % Y, zl

    return permuted(values, move)


def to_z_partner(values):
    def move(zh, c, x, y, zl):
        step = 1 if (zl == 0) == (c == 0) else -1
        z = (zh * ZL + zl + step) % (ZH * ZL)
        return z // ZL, c, x, y, z % ZL

    return permuted(values, move)


def z_groups():
    groups = []
    for c in range(CORE):
        for x in range(X):
            for y in range(Y):
                groups.append([flat(zh, c, x, y, zl) for zh in range(ZH) for zl in range(ZL)])
    return groups


def place():
    node, group = lax.axis_index("node"), lax.axis_index("group")
    core = lax.rem(node, CORE)
    x, y = lax.div(group, Y * ZL), lax.rem(lax.div(group, ZL), Y)
    return core, jnp.where(core == 0, x, y), jnp.where(core == 0, y, x), lax.rem(group, ZL)


SENT, KEPT = "sent", "kept"


def shape_of(what, rows):
    if what in (SENT, KEPT):
        return (ZH, X, Y, ZL, rows, QB)
    return (ZH, RING, ZL, PLAIN, rows, QB)


def slabs_of(what):
    return X * Y * ZL if what in (SENT, KEPT) else RING * ZL * PLAIN


def fetch(grads, what, half, at, zl, zh, target, sem):
    if what in (SENT, KEPT):
        slab = PLAIN + (1 - zl if what == SENT else zl)
        copy = pltpu.make_async_copy(grads.at[zh, half, :, :, :, slab], target, sem)
        copy.start()
        return copy
    copy = pltpu.make_async_copy(grads.at[zh, half, at, :, :, pl.ds(0, PLAIN)], target, sem)
    along_y = pltpu.make_async_copy(grads.at[zh, half, :, at, :, pl.ds(0, PLAIN)], target, sem)
    pl.when(half == 0)(copy.start)
    pl.when(half != 0)(along_y.start)
    return copy


def fetch_all(grads, steps, half, first, zl, helds, sems, skip=0):
    copies = []
    for k, what in enumerate(steps):
        at = first if what in (SENT, KEPT) else lax.rem(first + what, RING)
        for zh in range(ZH):
            copies.append(fetch(grads, what, half, at, zl, zh, helds[k].at[zh], sems.at[skip + k, zh]))
    return copies


def cast_kernel(groups, kept, grads, *refs):
    outs, refs = refs[: len(groups)], refs[len(groups) :]
    keeps, helds, sems = refs[: len(kept)], refs[len(kept) : -1], refs[-1]
    core, first, second, zl = place()
    steps = [what for group in groups for what in group]
    copies = iter(
        fetch_all(grads, steps, 1 - core, second, zl, helds, sems)
        + fetch_all(grads, kept, core, first, zl, keeps, sems, len(steps))
    )
    helds = iter(helds)
    for group, out in zip(groups, outs):
        begin = 0
        for what in group:
            held, end = next(helds), begin + slabs_of(what)
            for zh in range(ZH):
                next(copies).wait()
                out[zh, begin:end] = held[zh].reshape(end - begin, *held.shape[-2:]).astype(out.dtype)
            begin = end
    for copy in copies:
        copy.wait()


def add_kept_kernel(group, received, *refs):
    keeps, outs = refs[: len(group)], refs[len(group) :]
    begin = 0
    for what, kept, out in zip(group, keeps, outs):
        end = begin + slabs_of(what)
        for zh in range(ZH):
            out[zh] = (kept[zh] + received[zh, begin:end].reshape(kept.shape[1:]).astype(F32)).astype(out.dtype)
        begin = end


def add_kernel(group, grads, received, *refs):
    outs, helds, sems = refs[: len(group)], refs[len(group) : -1], refs[-1]
    core, first, _, zl = place()
    copies = iter(fetch_all(grads, group, core, first, zl, helds, sems))
    begin = 0
    for what, out, held in zip(group, outs, helds):
        end = begin + slabs_of(what)
        for zh in range(ZH):
            next(copies).wait()
            value = held[zh] + received[zh, begin:end].reshape(held.shape[1:]).astype(F32)
            out[zh] = value.astype(out.dtype)
        begin = end


VMEM = pl.BlockSpec(memory_space=pltpu.VMEM)
PARAMS = pltpu.CompilerParams(vmem_limit_bytes=10 * 1024 * 1024)
COST = pl.CostEstimate(flops=0, bytes_accessed=0, transcendentals=0)


def in_vmem(values):
    return pltpu.with_memory_space_constraint(values, pltpu.VMEM)


def run_on_grads(kernel, grads, steps, out_shape, received=(), kept=()):
    rows = grads.shape[-2]
    return pl.pallas_call(
        kernel,
        out_shape=out_shape,
        in_specs=[pl.BlockSpec(memory_space=pltpu.HBM)] + [VMEM] * len(received),
        out_specs=[VMEM] * len(out_shape),
        scratch_shapes=[pltpu.VMEM(shape_of(what, rows), F32) for what in steps]
        + [pltpu.SemaphoreType.DMA((len(steps) + len(kept), ZH))],
        compiler_params=PARAMS,
        cost_estimate=COST,
    )(pltpu.with_memory_space_constraint(grads, pltpu.HBM), *received)


def run_cast(grads, groups, kept):
    rows = grads.shape[-2]
    out_shape = [pltpu.VMEM((ZH, sum(map(slabs_of, group)), rows, QB), BF16) for group in groups]
    out_shape += [pltpu.VMEM(shape_of(what, rows), F32) for what in kept]
    steps = [what for group in groups for what in group]
    return run_on_grads(functools.partial(cast_kernel, groups, kept), grads, steps, out_shape, kept=kept)


def add_shape(group, rows):
    return [pltpu.VMEM(shape_of(what, rows), F32 if what in (0, KEPT) else BF16) for what in group]


def run_add(grads, group, received):
    return run_on_grads(functools.partial(add_kernel, group), grads, group, add_shape(group, grads.shape[-2]), [received])


def run_add_kept(group, received, keeps):
    return pl.pallas_call(
        functools.partial(add_kept_kernel, group),
        out_shape=add_shape(group, received.shape[-2]),
        in_specs=[VMEM] * (1 + len(keeps)),
        out_specs=[VMEM] * len(group),
        compiler_params=PARAMS,
        cost_estimate=COST,
    )(received, *keeps)


def paired_kernel(kept, arrived, *outs):
    core, first, _, _ = place()
    for shift, out in enumerate(outs):
        at = lax.rem(first + shift, RING)
        for zh in range(ZH):
            for other in range(RING):
                x, y = jnp.where(core == 0, at, other), jnp.where(core == 0, other, at)
                out[zh, other] = (kept[zh, x, y] + arrived[zh, x, y].astype(F32)).astype(out.dtype)


def run_paired(kept, arrived):
    rows = kept.shape[-2]
    return pl.pallas_call(
        paired_kernel,
        out_shape=[pltpu.VMEM((ZH, RING, ZL, rows, QB), BF16 if shift else F32) for shift in range(RING)],
        in_specs=[VMEM] * 2,
        out_specs=[VMEM] * RING,
        compiler_params=PARAMS,
        cost_estimate=COST,
    )(kept, in_vmem(arrived))


def plain_kernel(own, p1, p2, p3, out):
    for zh in range(ZH):
        out[zh] = own[zh] + p1[zh].astype(F32) + p2[zh].astype(F32) + p3[zh].astype(F32)


def run_plain(own, arrived):
    return pl.pallas_call(
        plain_kernel,
        out_shape=pltpu.VMEM(own.shape, F32),
        in_specs=[VMEM] * 4,
        out_specs=VMEM,
        compiler_params=PARAMS,
        cost_estimate=COST,
    )(own, *map(in_vmem, arrived))


def pieces_kernel(plain, own, p1, p2, p3, *outs):
    second = place()[2]
    for shift, out in enumerate(outs):
        other = lax.rem(second + shift, RING)
        for zh in range(ZH):
            paired = own[zh, other] + p1[zh, other].astype(F32) + p2[zh, other].astype(F32) + p3[zh, other].astype(F32)
            out[zh, :, 0:PLAIN] = plain[zh, other].astype(out.dtype)
            out[zh, :, PLAIN] = paired.astype(out.dtype)


def run_pieces(plain, own, arrived):
    rows = own.shape[-2]
    return pl.pallas_call(
        pieces_kernel,
        out_shape=[pltpu.VMEM((ZH, ZL, PLAIN + 1, rows, QB), BF16 if shift else F32) for shift in range(RING)],
        in_specs=[VMEM] * 5,
        out_specs=[VMEM] * RING,
        compiler_params=PARAMS,
        cost_estimate=COST,
    )(plain, own, *map(in_vmem, arrived))


def on_device(grads):
    rows = grads.shape[1] // (ZH * CORE * X * Y * ZL * SLABS * QB)
    grads = grads.reshape(ZH, CORE, X, Y, ZL, SLABS, rows, QB)
    groups = ((SENT, 2), (1, 3), (0, KEPT))
    outs = run_cast(grads, groups[:1], ())
    grads = lax.optimization_barrier((grads, *outs))[0]
    crossed = [to_other_core(out) for out in outs]
    outs = run_cast(grads, groups[1:], groups[0])
    grads = lax.optimization_barrier((grads, *outs))[0]
    crossed += [to_other_core(out) for out in outs[:2]]
    arrived, own = {}, {}
    for group, received in zip(groups, crossed):
        summed = run_add(grads, group, received) if group != groups[0] else run_add_kept(group, received, outs[2:])
        grads = lax.optimization_barrier((grads, *summed))[0]
        for what, out in zip(group, summed):
            if what == SENT:
                arrived[what] = to_z_partner(out)
            elif what in (0, KEPT):
                own[what] = out
            else:
                arrived[what] = along(out, what, True)

    paired = run_paired(own[KEPT], arrived[SENT])
    paired_arrived = {shift: along(paired[shift], shift, True) for shift in (1, 3, 2)}
    plain = run_plain(own[0], [arrived[shift] for shift in (2, 1, 3)])
    pieces = run_pieces(plain, paired[0], [paired_arrived[shift] for shift in (2, 1, 3)])
    summed = pieces[0]
    for shift in (2, 1, 3):
        summed += along(pieces[shift], shift, False).astype(F32)
    pieces = summed.astype(BF16).reshape(ZH * ZL, PLAIN + 1, rows, QB)
    pieces = lax.all_to_all(pieces, AXES, 0, 0, axis_index_groups=z_groups(), tiled=True).astype(F32)
    of_plain = jnp.sum(pieces[:, :PLAIN], axis=0)
    of_paired = jnp.sum(pieces[:, PLAIN].reshape(ZH, ZL, rows, QB), axis=0)
    return jnp.concatenate([of_plain, of_paired]).reshape(SLABS * rows * QB)


def solution(mesh):
    placed = (P(("node", "group"), None),)
    return jax.shard_map(
        on_device, mesh=mesh, in_specs=placed, out_specs=P(("node", "group")), check_vma=False
    )
```
